32 devices in a mesh: hop: 8 (over z, y), tensor: 4 (over x, core).
Axes of the slice: x: 2, y: 2, z: 4, core: 2. Of those that a mesh axis runs over, the one named last changes fastest.
Arguments:
- tokens: bfloat16 [3, 2048, 1024], P(None, 'hop', 'tensor'), may hold values from -17 to 17
- targets: bfloat16 [2, 2048, 1024], P(None, 'hop', 'tensor'), may hold values from -6 to 6
- w_in: bfloat16 [8, 1024, 32768], P('hop', None, 'tensor'), may hold values from -0.1875 to 0.1875
- w_out: bfloat16 [32768, 1024], P('tensor', 'hop'), may hold values from -0.03125 to 0.03125
- noise_field: bfloat16 [8, 1024, 32768], P('hop', None, 'tensor'), may hold values from -18 to 18
- step_size: float32 [8], replicated, may hold values from 0.005 to 0.02
- clip_ratio: float32 [8], replicated, may hold values from 0.5 to 2
- noise_mult: float32 [8], replicated, may hold values from 0.002 to 0.02
- plan: int32 [8], replicated, may hold values from 0 to 7, each once
- live_rows: int32 [2, 8], P(None, 'hop'), may hold values from 128 to 256
Outputs:
- predictions: bfloat16 [2048, 1024], P('hop', 'tensor')
- row_losses: float32 [2, 2048], P(None, 'hop')
The draws below stay inside these ranges and needn't reach their ends.
Inputs may be any that keep to these rules, and one draw needn't show every extreme that they name: `plan`: each configuration names the partition that holds it in round two; every partition is named once. The first live_rows[k, g] rows of partition g are live in round k.
All inputs are finite; a program needn't handle non-finite values.
Results may differ from the reference program's by a relative error of at most 0.0085.
Values may be sent and summed in bfloat16 or wider, within the bound.
A program may use at most 192 MiB of HBM per device.

```python
import math
import jax
import jax.numpy as jnp
from jax import lax

D = 1024
FF = 32768
ROWS = 256
CONFIGS = 8
ALL_ROWS = 2048


def draw_tokens(key, part):
    first_key, second_key = jax.random.split(jax.random.fold_in(key, 11))
    entries = jnp.clip(jax.random.normal(first_key, (3, ALL_ROWS, D), jnp.float32), -5.0, 5.0)
    scales = jnp.exp(jax.random.uniform(second_key, (3, ALL_ROWS, 1), jnp.float32, math.log(0.33), math.log(3.3)))
    return (entries * scales).astype(jnp.bfloat16)


def draw_noise_field(key, part):
    first_key = jax.random.fold_in(key, 23)
    columns = jnp.arange(FF, dtype=jnp.float32) / FF
    entries = jnp.clip(jax.random.normal(first_key, (CONFIGS, D, FF), jnp.float32), -5.0, 5.0)
    scales = jnp.power(3.0, columns)[None, None, :]
    return (entries * scales).astype(jnp.bfloat16)


def plant(values, rng, least, top_value):
    index_at = [jax.random.randint(jax.random.fold_in(rng, axis), (), 0, length) for axis, length in enumerate(values.shape)]
    widest = values.shape.index(max(values.shape))
    beside = index_at[:widest] + [(index_at[widest] + 1) % values.shape[widest]] + index_at[widest + 1:]
    return values.at[tuple(index_at)].set(least).at[tuple(beside)].set(top_value)


def shard_levels(stream_key, extent, cuts, low, top_value):
    level = 1.0
    for position, blocks in cuts:
        draws = jax.random.uniform(jax.random.fold_in(jax.random.fold_in(stream_key, 6), position), (blocks,), jnp.float32, low / len(cuts), top_value / len(cuts))
        level = level * jnp.repeat(jnp.exp(draws), extent[position] // blocks).reshape((-1,) + (1,) * (len(extent) - 1 - position))
    return level


def normal_values(stream_key, shape, scale, most, cuts=(), kind=jnp.bfloat16):
    values = scale * jax.random.normal(stream_key, shape, jnp.float32)
    if cuts:
        values = values * shard_levels(stream_key, shape, cuts, -0.22, 0.18)
    return jnp.clip(values, -most, most).astype(kind)


def setup_inputs(seed: int = 0) -> dict:
    keys = jax.random.split(jax.random.key(seed), 11)
    return {
        "tokens": draw_tokens(jax.random.fold_in(keys[10], 71), 0),
        "targets": normal_values(keys[1], (2, ALL_ROWS, D), 1.0, 6.0, ((1, 8), (2, 4))),
        "w_in": normal_values(keys[2], (CONFIGS, D, FF), D ** -0.5, 0.1875, ((0, 8), (2, 4))),
        "w_out": normal_values(keys[3], (FF, D), FF ** -0.5, 0.03125, ((0, 4), (1, 8))),
        "noise_field": draw_noise_field(jax.random.fold_in(keys[10], 71), 0),
        "step_size": jnp.clip(jnp.exp(jax.random.uniform(keys[5], (CONFIGS,), jnp.float32, math.log(0.005), math.log(0.02))), 0.005, 0.02),
        "clip_ratio": jnp.clip(jnp.exp(jax.random.uniform(keys[6], (CONFIGS,), jnp.float32, math.log(0.5), math.log(2.0))), 0.5, 2.0),
        "noise_mult": jnp.clip(jnp.exp(jax.random.uniform(keys[7], (CONFIGS,), jnp.float32, math.log(0.002), math.log(0.02))), 0.002, 0.02),
        "plan": jax.random.permutation(keys[8], CONFIGS).astype(jnp.int32),
        "live_rows": plant(jax.random.randint(keys[9], (2, CONFIGS), ROWS // 2, ROWS + 1), jax.random.fold_in(keys[9], 1), ROWS // 2, ROWS).astype(jnp.int32),
    }


def gelu_parts(pre_act):
    inside = 0.7978845608 * (pre_act + 0.044715 * pre_act * pre_act * pre_act)
    tangent = jnp.tanh(inside)
    output = 0.5 * pre_act * (1.0 + tangent)
    slope_value = 0.5 * (1.0 + tangent) + 0.5 * pre_act * (1.0 - tangent * tangent) * 0.7978845608 * (1.0 + 0.134145 * pre_act * pre_act)
    return (output, slope_value)

def train_round(weights, inputs, wanted, noise_block, live_count, learn_rate, clip_share, noise_scale, w_out):
    pre_act = jnp.dot(inputs, weights, preferred_element_type=jnp.float32)
    output, slope_value = gelu_parts(pre_act)
    active = output.astype(jnp.bfloat16)
    result = jnp.dot(active, w_out, preferred_element_type=jnp.float32)
    differ = result - wanted.astype(jnp.float32)
    live_mask = (jnp.arange(inputs.shape[0], dtype=jnp.int32) < live_count).astype(jnp.float32)
    losses = 0.5 * lax.optimization_barrier(jnp.sum(differ * differ, axis=1)) * live_mask
    backed = differ.astype(jnp.bfloat16)
    grad_act = jnp.dot(backed, w_out.T, preferred_element_type=jnp.float32) * slope_value
    input_square = lax.optimization_barrier(jnp.sum(jnp.square(inputs.astype(jnp.float32)), axis=1))
    grad_square = lax.optimization_barrier(jnp.sum(grad_act * grad_act, axis=1))
    row_norms = jnp.sqrt(input_square * grad_square)
    clip_level = clip_share * jnp.sum(row_norms * live_mask) / live_count.astype(jnp.float32)
    factor = live_mask * jnp.minimum(1.0, clip_level / (row_norms + 1e-06))
    scaled = (grad_act * factor[:, None]).astype(jnp.bfloat16)
    update = jnp.dot(inputs.T, scaled, preferred_element_type=jnp.float32) + noise_scale * clip_level * noise_block.astype(jnp.float32)
    spread = jnp.mean(update * update)
    renewed = (weights.astype(jnp.float32) - learn_rate * update * lax.rsqrt(spread + 1e-06)).astype(jnp.bfloat16)
    return (renewed, losses)

def reference(tokens, targets, w_in, w_out, noise_field, step_size, clip_ratio, noise_mult, plan, live_rows):
    split_tokens = tokens.reshape(3, CONFIGS, ROWS, D)
    split_targets = targets.reshape(2, CONFIGS, ROWS, D)

    def round_step(members):
        return train_round(members[0], members[1], members[2], members[3], members[4], members[5], members[6], members[7], w_out)
    trained_one, loss_one = lax.map(round_step, (w_in, split_tokens[0], split_targets[0], noise_field, live_rows[0], step_size, clip_ratio, noise_mult))
    indices = jnp.arange(CONFIGS, dtype=jnp.int32)
    owners = lax.optimization_barrier(jnp.sum(indices[:, None] * (plan[:, None] == indices[None, :]).astype(jnp.int32), axis=0)).astype(jnp.int32)
    arrived = jnp.take(trained_one, owners, axis=0)
    trained_two, loss_two = lax.map(round_step, (arrived, split_tokens[1], split_targets[1], noise_field, live_rows[1], jnp.take(step_size, owners), jnp.take(clip_ratio, owners), jnp.take(noise_mult, owners)))

    def evaluate(members):
        pre_act = jnp.dot(members[1], members[0], preferred_element_type=jnp.float32)
        output, slope_value = gelu_parts(pre_act)
        return jnp.dot(output.astype(jnp.bfloat16), w_out, preferred_element_type=jnp.float32).astype(jnp.bfloat16)
    predictions = lax.map(evaluate, (trained_two, split_tokens[2])).reshape(CONFIGS * ROWS, D)
    row_losses = jnp.stack([loss_one.reshape(-1), loss_two.reshape(-1)])
    return (predictions, row_losses)
```

```python
import jax
import jax.numpy as jnp
from jax import lax
from jax.sharding import PartitionSpec as P

BF = jnp.bfloat16
F32 = jnp.float32


def gelu_parts(pre_act):
    inside = 0.7978845608 * (pre_act + 0.044715 * pre_act * pre_act * pre_act)
    tangent = jnp.tanh(inside)
    output = 0.5 * pre_act * (1.0 + tangent)
    slope_value = 0.5 * (1.0 + tangent) + 0.5 * pre_act * (
        1.0 - tangent * tangent
    ) * 0.7978845608 * (1.0 + 0.134145 * pre_act * pre_act)
    return (output, slope_value)


def dot(a, b):
    return jnp.dot(a, b, preferred_element_type=F32)


def row_products(a, b):
    return lax.dot_general(a, b, (((1,), (1,)), ((), ())), preferred_element_type=F32)


def fine_dot(gram, b):
    high = gram.astype(BF)
    low = (gram - high.astype(F32)).astype(BF)
    both = dot(jnp.concatenate([high, low], axis=1), jnp.concatenate([b, b], axis=0))
    return both


def pick(array, index):
    return lax.dynamic_index_in_dim(array, index, 0, keepdims=False)


def local(
    tokens, targets, w_in, w_out, noise_field, step_size, clip_ratio, noise_mult, plan, live_rows
):
    hops = plan.shape[0]
    me = lax.axis_index("hop")
    rows, cols = tokens.shape[1], w_in.shape[2]
    weights, noise = w_in[0], noise_field[0]
    indices = jnp.arange(hops, dtype=jnp.int32)
    owners = jnp.sum(
        indices[:, None] * (plan[:, None] == indices[None, :]).astype(jnp.int32), axis=0
    )
    goes_to = pick(plan, me)
    holder = pick(owners, me)

    own = lax.all_gather(tokens, "tensor", axis=2, tiled=True)
    near = jnp.concatenate([tokens[1:], targets[1:]], axis=0)
    theirs = pick(lax.all_gather(near, "hop", axis=0), goes_to)
    next_rows = lax.all_gather(theirs[:2], "tensor", axis=2, tiled=True)
    next_wanted = theirs[2]
    all_w_out = lax.all_gather(w_out, "hop", axis=1, tiled=True)

    depth = own.shape[2]
    travels = dot(own[1:].reshape(2 * rows, depth), noise).astype(BF)
    block = 2 * rows // hops
    spread_out = lax.all_to_all(
        travels.reshape(hops, block, cols), "hop", split_axis=0, concat_axis=0, tiled=True
    )
    ordered = jnp.stack([pick(spread_out, plan[c]) for c in range(hops)])
    arrived = lax.all_to_all(ordered, "hop", split_axis=0, concat_axis=0, tiled=True)
    arrived = arrived.reshape(2, rows, cols)

    noise_square = jnp.sum(jnp.square(noise.astype(F32)))
    facts = jnp.stack([live_rows[1, 0].astype(F32), noise_square])
    next_facts = pick(lax.all_gather(facts, "hop", axis=0), goes_to)

    first = own[0]
    second, third = next_rows[0], next_rows[1]
    stacked = jnp.concatenate([first, second, third], axis=0)
    by_weights = dot(stacked, weights)
    by_noise = dot(stacked, noise)

    learn_rate, clip_share, noise_scale = (
        pick(step_size, me),
        pick(clip_ratio, me),
        pick(noise_mult, me),
    )
    entries = depth * cols * lax.axis_size("tensor")

    def forward(active):
        return lax.psum_scatter(dot(active, all_w_out), "tensor", scatter_dimension=1, tiled=True)

    def train(pre_act, inputs, wanted, live_count, noise_products, noise_energy):
        output, slope_value = gelu_parts(pre_act)
        differ = forward(output.astype(BF)) - wanted.astype(F32)
        live_mask = (jnp.arange(rows, dtype=jnp.int32) < live_count).astype(F32)
        loss_part = 0.5 * jnp.sum(differ * differ, axis=1)
        backed = lax.all_gather(differ.astype(BF), "tensor", axis=1, tiled=True)
        grad_act = row_products(backed, all_w_out) * slope_value
        grad_part = jnp.sum(grad_act * grad_act, axis=1)
        sums = lax.psum(jnp.stack([loss_part, grad_part]), "tensor")
        input_square = jnp.sum(jnp.square(inputs.astype(F32)), axis=1)
        row_norms = jnp.sqrt(input_square * sums[1])
        clip_level = clip_share * jnp.sum(row_norms * live_mask) / live_count.astype(F32)
        factor = live_mask * jnp.minimum(1.0, clip_level / (row_norms + 1e-06))
        scaled = (grad_act * factor[:, None]).astype(BF)
        level = noise_scale * clip_level
        inner = fine_dot(row_products(inputs, inputs), scaled)
        wide = scaled.astype(F32)
        part = jnp.sum(wide * (inner + (2.0 * level) * noise_products.astype(F32)))
        spread = lax.psum(part + level * level * noise_energy, "tensor") / entries
        step = learn_rate * lax.rsqrt(spread + 1e-06)
        return scaled, level, step, sums[0] * live_mask

    scaled_one, level_one, step_one, loss_one = train(
        by_weights[:rows], first, targets[0], live_rows[0, 0], by_noise[:rows], noise_square
    )
    moved = fine_dot(row_products(stacked[rows:], first), scaled_one)
    pre_both = by_weights[rows:] - step_one * (moved + level_one * by_noise[rows:])
    scaled_two, level_two, step_two, loss_two = train(
        pre_both[:rows],
        second,
        next_wanted,
        next_facts[0].astype(jnp.int32),
        arrived[0],
        next_facts[1],
    )
    moved = fine_dot(row_products(third, second), scaled_two)
    pre_eval = pre_both[rows:] - step_two * (moved + level_two * arrived[1].astype(F32))
    output, slope_value = gelu_parts(pre_eval)
    outcome = forward(output.astype(BF)).astype(BF)
    predictions = pick(lax.all_gather(outcome, "hop", axis=0), holder)
    loss_two = pick(lax.all_gather(loss_two, "hop", axis=0), holder)
    return (predictions, jnp.stack([loss_one, loss_two]))


def solution(mesh):
    return jax.shard_map(
        local,
        mesh=mesh,
        in_specs=(
            P(None, "hop", "tensor"),
            P(None, "hop", "tensor"),
            P("hop", None, "tensor"),
            P("tensor", "hop"),
            P("hop", None, "tensor"),
            P(),
            P(),
            P(),
            P(),
            P(None, "hop"),
        ),
        out_specs=(P("hop", "tensor"), P(None, "hop")),
        check_vma=False,
    )
```

```python
import jax
import jax.numpy as jnp
from jax import lax
from jax.experimental import pallas as pl
from jax.experimental.pallas import tpu as pltpu
from jax.sharding import PartitionSpec as P

BF = jnp.bfloat16
F32 = jnp.float32


def gelu_parts(pre_act):
    inside = 0.7978845608 * (pre_act + 0.044715 * pre_act * pre_act * pre_act)
    tangent = jnp.tanh(inside)
    output = 0.5 * pre_act * (1.0 + tangent)
    slope_value = 0.5 * (1.0 + tangent) + 0.5 * pre_act * (
        1.0 - tangent * tangent
    ) * 0.7978845608 * (1.0 + 0.134145 * pre_act * pre_act)
    return (output, slope_value)


def dot(a, b):
    return jnp.dot(a, b, preferred_element_type=F32)


def row_products(a, b):
    return lax.dot_general(a, b, (((1,), (1,)), ((), ())), preferred_element_type=F32)


def fine_dot(gram, b):
    high = gram.astype(BF)
    low = (gram - high.astype(F32)).astype(BF)
    both = dot(jnp.concatenate([high, low], axis=1), jnp.concatenate([b, b], axis=0))
    return both


SLAB = 16


def three_parts(values):
    high = values.astype(BF)
    rest = values - high.astype(F32)
    middle = rest.astype(BF)
    return [high, middle, (rest - middle.astype(F32)).astype(BF)]


def after(array, other):
    return lax.optimization_barrier((array, other))[0]


def copy_block(order_ref, in_ref, out_ref):
    out_ref[...] = in_ref[...]


def reorder(blocks, order):
    block = (1,) + blocks.shape[1:]
    return pl.pallas_call(
        copy_block,
        out_shape=jax.ShapeDtypeStruct(blocks.shape, blocks.dtype),
        grid_spec=pltpu.PrefetchScalarGridSpec(
            num_scalar_prefetch=1,
            grid=(blocks.shape[0],),
            in_specs=[pl.BlockSpec(block, lambda i, order_ref: (order_ref[i], 0, 0))],
            out_specs=pl.BlockSpec(block, lambda i, order_ref: (i, 0, 0)),
        ),
    )(order, blocks)


def route(blocks, plan):
    spread = lax.all_to_all(blocks, "hop", split_axis=0, concat_axis=0, tiled=True)
    return lax.all_to_all(reorder(spread, plan), "hop", split_axis=0, concat_axis=0, tiled=True)


def pick(array, index):
    return lax.dynamic_index_in_dim(array, index, 0, keepdims=False)


def local(
    tokens, targets, w_in, w_out, noise_field, step_size, clip_ratio, noise_mult, plan, live_rows
):
    hops = plan.shape[0]
    me = lax.axis_index("hop")
    rows, cols = tokens.shape[1], w_in.shape[2]
    weights, noise = w_in[0], noise_field[0]
    indices = jnp.arange(hops, dtype=jnp.int32)
    owners = jnp.sum(
        indices[:, None] * (plan[:, None] == indices[None, :]).astype(jnp.int32), axis=0
    )
    holder = pick(owners, me)

    all_w_out = lax.all_gather(w_out, "hop", axis=1, tiled=True)

    def widen(block):
        return lax.all_gather(block, "tensor", axis=1, tiled=True)

    own_second = widen(tokens[1])
    own_third = widen(after(tokens[2], own_second))
    first = widen(after(tokens[0], own_third))
    depth = first.shape[1]

    noise_square = jnp.sum(jnp.square(noise.astype(F32)))
    facts = jnp.stack(three_parts(jnp.stack([live_rows[1, 0].astype(F32), noise_square])))
    slab = jnp.zeros((hops, SLAB, tokens.shape[2]), BF).at[:, :3, :2].set(facts[None])
    near = jnp.concatenate([tokens[1:], targets[1:]], axis=0).reshape(hops, -1, tokens.shape[2])
    depth_near = near.shape[1]
    landed = route(jnp.concatenate([near, slab], axis=1), plan)
    next_facts = jnp.sum(landed[0, depth_near : depth_near + 3, :2].astype(F32), axis=0)
    theirs = landed[:, :depth_near].reshape(3, rows, tokens.shape[2])
    next_wanted = theirs[2]

    def products(own):
        return dot(own, noise).astype(BF).reshape(hops, rows // hops, cols)

    arrived = [route(products(own), plan).reshape(rows, cols) for own in (own_second, own_third)]

    second = widen(theirs[0])
    third = widen(after(theirs[1], second))
    by_weights_first, by_noise_first = dot(first, weights), dot(first, noise).astype(BF)
    later = jnp.concatenate([second, third], axis=0)
    by_weights, by_noise = dot(later, weights), dot(later, noise)

    learn_rate, clip_share, noise_scale = (
        pick(step_size, me),
        pick(clip_ratio, me),
        pick(noise_mult, me),
    )
    entries = depth * cols * lax.axis_size("tensor")

    def forward(active):
        return lax.psum_scatter(dot(active, all_w_out), "tensor", scatter_dimension=1, tiled=True)

    def train(pre_act, inputs, wanted, live_count, noise_products, noise_energy):
        output, slope_value = gelu_parts(pre_act)
        differ = forward(output.astype(BF)) - wanted.astype(F32)
        live_mask = (jnp.arange(rows, dtype=jnp.int32) < live_count).astype(F32)
        loss_part = 0.5 * jnp.sum(differ * differ, axis=1)
        backed = lax.all_gather(differ.astype(BF), "tensor", axis=1, tiled=True)
        grad_act = row_products(backed, all_w_out) * slope_value
        grad_part = jnp.sum(grad_act * grad_act, axis=1)
        sums = lax.psum(jnp.stack([loss_part, grad_part]), "tensor")
        input_square = jnp.sum(jnp.square(inputs.astype(F32)), axis=1)
        row_norms = jnp.sqrt(input_square * sums[1])
        clip_level = clip_share * jnp.sum(row_norms * live_mask) / live_count.astype(F32)
        factor = live_mask * jnp.minimum(1.0, clip_level / (row_norms + 1e-06))
        scaled = (grad_act * factor[:, None]).astype(BF)
        level = noise_scale * clip_level
        inner = fine_dot(row_products(inputs, inputs), scaled)
        wide = scaled.astype(F32)
        part = jnp.sum(wide * (inner + (2.0 * level) * noise_products.astype(F32)))
        spread = lax.psum(part + level * level * noise_energy, "tensor") / entries
        step = learn_rate * lax.rsqrt(spread + 1e-06)
        return scaled, level, step, sums[0] * live_mask

    scaled_one, level_one, step_one, loss_one = train(
        by_weights_first, first, targets[0], live_rows[0, 0], by_noise_first, noise_square
    )
    moved = fine_dot(row_products(later, first), scaled_one)
    pre_both = by_weights - step_one * (moved + level_one * by_noise)
    scaled_two, level_two, step_two, loss_two = train(
        pre_both[:rows],
        second,
        next_wanted,
        next_facts[0].astype(jnp.int32),
        arrived[0],
        next_facts[1],
    )
    moved = fine_dot(row_products(third, second), scaled_two)
    pre_eval = pre_both[rows:] - step_two * (moved + level_two * arrived[1].astype(F32))
    output, slope_value = gelu_parts(pre_eval)
    outcome = forward(output.astype(BF)).astype(BF)
    width = outcome.shape[1]
    losses = jnp.concatenate([p.reshape(-1, width) for p in three_parts(loss_two)], axis=0)
    count = losses.shape[0]
    losses = jnp.pad(losses, ((0, -count % SLAB), (0, 0)))
    back = pick(lax.all_gather(jnp.concatenate([outcome, losses], axis=0), "hop", axis=0), holder)
    predictions = back[:rows]
    loss_back = back[rows : rows + count].astype(F32).reshape(3, rows)
    return (predictions, jnp.stack([loss_one, jnp.sum(loss_back, axis=0)]))


def solution(mesh):
    return jax.shard_map(
        local,
        mesh=mesh,
        in_specs=(
            P(None, "hop", "tensor"),
            P(None, "hop", "tensor"),
            P("hop", None, "tensor"),
            P("tensor", "hop"),
            P("hop", None, "tensor"),
            P(),
            P(),
            P(),
            P(),
            P(None, "hop"),
        ),
        out_specs=(P("hop", "tensor"), P(None, "hop")),
        check_vma=False,
    )
```
